128 devices in a mesh: row: 8 (over x, core), col: 16 (over y, z).
Axes of the slice: x: 4, y: 4, z: 4, core: 2. Of those that a mesh axis runs over, the one named last changes fastest.
Arguments:
- eigvec_slab: bfloat16 [512, 131072], P('col', 'row'), may hold values from -1 to 1
- occupations: int32 [512], replicated, may hold values from 1 to 2
- energies: float32 [512], replicated, may hold values from -1.6 to -0.1
- tile_owner: int32 [2048], P(('row', 'col')), may hold values from -1 to 15, as said below
- margin_change: bfloat16 [4096, 3, 64, 128], P(('row', 'col')), may hold values from -0.23925781 to 0.23925781
- hamiltonian_change: bfloat16 [4096, 3, 64, 128], P(('row', 'col')), may hold values from -0.23925781 to 0.23925781
- basis_atom: int32 [131072], replicated, may hold values from 0 to 20479, as said below
Outputs:
- forces: float32 [3, 20480], P(None, ('row', 'col'))
The draws below stay inside these ranges and needn't reach their ends.
Inputs may be any that keep to these rules, and one draw needn't show every extreme that they name: `tile_owner`: owners lie in the sending device's row; at most 2 row blocks of one device share an owner, and some device gives 2 to one owner. -1 marks a block outside the sparsity pattern. `basis_atom`: the basis functions of device d (functions d * 64 * 16 onward) belong to atoms d * 160 to (d + 1) * 160 - 1; ids never fall, every atom has 1 to 12 basis functions, and on every device one atom has exactly 12.
All inputs are finite; a program needn't handle non-finite values.
Results may differ from the reference program's by a relative error of at most 0.0035.
Values may be sent and summed in bfloat16 or wider, within the bound.
No kernel may reach another device: no remote copies, remote signals or barrier semaphores. Data moves between devices by JAX's collectives and lax.ppermute only.
A program may use at most 64 MiB of HBM per device.

```python
import jax
import jax.numpy as jnp
from jax import lax

STATES = 512
PANEL = 128
BLOCK_ROWS = 64
BLOCKS_DEV = 16
CAP = 2
ATOMS_DEV = 160
BASIS = 131072
ATOMS = 20480
SLOTS = 32
N_ROW = 8
N_COL = 16
DEVICES = 128


def draw_tile_owner(key, part):
    key = jax.random.fold_in(key, 11)
    key_perm, key_group, key_keep = jax.random.split(key, 3)
    groups = BLOCKS_DEV // 2
    half = groups // 2
    hotset = half
    source = jnp.arange(DEVICES, dtype=jnp.int32)
    column = source % N_COL
    rowpos = source // N_COL
    gindex = jnp.arange(groups, dtype=jnp.int32)
    spread = hotset + (column[:, None] + gindex[None, :]) % (N_COL - hotset)
    crowded = (column[:, None] + gindex[None, :]) % hotset
    target = jnp.where(gindex[None, :] < half, spread, crowded)
    row_perms = jax.vmap(lambda k: jax.random.permutation(k, N_COL))(jax.random.split(key_perm, N_ROW)).astype(jnp.int32)
    owner_group = jnp.take_along_axis(row_perms[rowpos], target, axis=1)
    group_perms = jax.vmap(lambda k: jax.random.permutation(k, groups))(jax.random.split(key_group, DEVICES)).astype(jnp.int32)
    owner_pair = jnp.take_along_axis(owner_group, group_perms, axis=1)
    keep = jax.random.randint(key_keep, (DEVICES, groups), 0, 4) > 0
    keep = keep.at[0].set(True)
    second = jnp.where(keep, owner_pair, -1)
    return jnp.stack([owner_pair, second], axis=2).reshape(DEVICES * BLOCKS_DEV).astype(jnp.int32)


def draw_basis_atom(key, part):
    key = jax.random.fold_in(key, 23)
    rows_dev = BLOCK_ROWS * BLOCKS_DEV
    spare = rows_dev - ATOMS_DEV - 11
    others = ATOMS_DEV - 1

    def one_device(dkey):
        key_perm, key_big = jax.random.split(dkey)
        order = jax.random.permutation(key_perm, others * 10).astype(jnp.int32)
        inverse = jnp.zeros((others * 10,), jnp.int32).at[order].set(jnp.arange(others * 10, dtype=jnp.int32))
        taken = (inverse < spare).astype(jnp.int32)
        more = jnp.sum(taken.reshape(others, 10), axis=1).astype(jnp.int32)
        rest = 1 + more
        big = jax.random.randint(key_big, (), 0, ATOMS_DEV).astype(jnp.int32)
        index = jnp.arange(ATOMS_DEV, dtype=jnp.int32)
        source = jnp.clip(jnp.where(index < big, index, index - 1), 0, others - 1)
        counts = jnp.where(index == big, 12, rest[source]).astype(jnp.int32)
        ends = jnp.cumsum(counts).astype(jnp.int32)
        place = jnp.arange(rows_dev, dtype=jnp.int32)
        return jnp.sum((place[:, None] >= ends[None, :]).astype(jnp.int32), axis=1).astype(jnp.int32)
    ids = jax.vmap(one_device)(jax.random.split(key, DEVICES))
    offset = jnp.arange(DEVICES, dtype=jnp.int32)[:, None] * ATOMS_DEV
    return (ids + offset).reshape(DEVICES * rows_dev).astype(jnp.int32)


def touch_ends(entries, key, least, high):
    shape = entries.shape
    index_at = [jax.random.randint(jax.random.fold_in(key, axis), (), 0, shape[axis]) for axis in range(len(shape))]
    entries = entries.at[tuple(index_at)].set(least)
    longest = shape.index(max(shape))
    index_at[longest] = (index_at[longest] + 1) % shape[longest]
    return entries.at[tuple(index_at)].set(high)


def level_of(rng, dims, pieces, least, top_value):
    gain, own = 1.0, jax.random.fold_in(rng, 6)
    for dim, parts in pieces:
        draws = jnp.exp(jax.random.uniform(jax.random.fold_in(own, dim), (parts,), jnp.float32, least / len(pieces), top_value / len(pieces)))
        gain = gain * jnp.repeat(draws, dims[dim] // parts).reshape([-1 if axis == dim else 1 for axis in range(len(dims))])
    return gain


def noise(own_key, extent, width, limit, pieces=(), held_as=jnp.bfloat16):
    drawn = jax.random.normal(own_key, extent, jnp.float32) * width
    if len(pieces) > 0:
        drawn = level_of(own_key, extent, pieces, -0.22, 0.18) * drawn
    return jnp.clip(drawn, min=-limit, max=limit).astype(held_as)


def setup_inputs(seed: int = 0) -> dict:
    keys = jax.random.split(jax.random.key(seed), 8)
    return {
        "eigvec_slab": noise(keys[0], (STATES, BASIS), 0.15, 1.0, ((0, 16), (1, 8))),
        "occupations": touch_ends(jax.random.randint(keys[1], (STATES,), 1, 3), jax.random.fold_in(keys[1], 1), 1, 2).astype(jnp.int32),
        "energies": jnp.clip(jax.random.uniform(keys[2], (STATES,), jnp.float32, -1.6, -0.1), -1.6, -0.1),
        "tile_owner": draw_tile_owner(jax.random.fold_in(keys[7], 71), 0),
        "margin_change": noise(keys[4], (DEVICES * SLOTS, 3, BLOCK_ROWS, PANEL), 0.04, 0.23925781, ((0, 128),)),
        "hamiltonian_change": noise(keys[5], (DEVICES * SLOTS, 3, BLOCK_ROWS, PANEL), 0.04, 0.23925781, ((0, 128),)),
        "basis_atom": draw_basis_atom(jax.random.fold_in(keys[7], 71), 0),
    }


def reference(eigvec_slab, occupations, energies, tile_owner, margin_change, hamiltonian_change, basis_atom):
    occ = occupations.astype(jnp.float32)
    eweight = occ * energies
    panel = eigvec_slab[:, :PANEL].astype(jnp.float32)
    weights = jnp.concatenate([(panel * occ[:, None]).astype(jnp.bfloat16), (panel * eweight[:, None]).astype(jnp.bfloat16)], axis=1)
    density = lax.dot_general(eigvec_slab, weights, (((0,), (0,)), ((), ())), preferred_element_type=jnp.float32).astype(jnp.bfloat16)
    owners = tile_owner.reshape(DEVICES, BLOCKS_DEV)
    same = owners[:, :, None] == owners[:, None, :]
    position = jnp.arange(BLOCKS_DEV, dtype=jnp.int32)
    lower = position[None, :] < position[:, None]
    rank = jnp.sum((same & lower[None]).astype(jnp.int32), axis=2).astype(jnp.int32)
    device = jnp.arange(DEVICES, dtype=jnp.int32)[:, None]
    row_index = device // N_COL
    col_index = device % N_COL
    live = owners >= 0
    slot = ((row_index * N_COL + owners) * N_COL + col_index) * CAP + rank
    slot = jnp.where(live, slot, 0).astype(jnp.int32)
    tiles = density.reshape(DEVICES, BLOCKS_DEV, BLOCK_ROWS, 2 * PANEL)

    def one_device(items):
        dtile, where_slot, alive = items
        ochange = margin_change[where_slot].astype(jnp.float32)
        hchange = hamiltonian_change[where_slot].astype(jnp.float32)
        pdens = dtile[..., :PANEL].astype(jnp.float32)
        wdens = dtile[..., PANEL:].astype(jnp.float32)
        frow = jnp.sum(pdens[:, None] * hchange - wdens[:, None] * ochange, axis=-1)
        return frow * alive.astype(jnp.float32)[:, None, None]

    frows = lax.map(one_device, (tiles, slot, live))
    frows = jnp.transpose(frows, (0, 1, 3, 2)).reshape(BASIS, 3)
    summed = jax.ops.segment_sum(frows, basis_atom, num_segments=ATOMS)
    return (2.0 * summed).T
```

```python
import jax
import jax.numpy as jnp
from jax import lax
from jax.experimental import pallas as pl
from jax.experimental.pallas import tpu as pltpu
from jax.sharding import PartitionSpec as P

ATOMS_DEV = 160
BF16 = jnp.bfloat16
F32 = jnp.float32
VMEM = pltpu.VMEM
SMEM = pltpu.SMEM


def whole(space=VMEM):
    return pl.BlockSpec(memory_space=space)


def slots_of(owner_ref, columns, blocks, shape):
    lane = lax.broadcasted_iota(jnp.int32, shape, 1)
    owner, rank = lane // 2, lane % 2
    first = jnp.full(shape, blocks, jnp.int32)
    last = jnp.full(shape, -1, jnp.int32)
    for b in range(blocks):
        last = jnp.where(owner == owner_ref[b], b, last)
        first = jnp.where(owner == owner_ref[blocks - 1 - b], blocks - 1 - b, first)
    second = jnp.where(last > first, last, blocks)
    return jnp.where(rank == 0, first, second)


def announce_kernel(owner_ref, panel_ref, out_ref):
    columns, _, width = out_ref.shape
    states = panel_ref.shape[0]
    out_ref[:, :states, :] = jnp.broadcast_to(panel_ref[...][None], (columns, states, width))
    table = slots_of(owner_ref, columns, owner_ref.shape[0], (16, width))
    out_ref[:, states:, :] = jnp.broadcast_to(table.astype(F32).astype(BF16)[None], (columns, 16, width))


def double_kernel(slab_ref, out_ref):
    columns, blocks, states, width = out_ref.shape
    blocks -= 1
    low = lax.broadcasted_iota(jnp.int32, (states, width), 1) < width // 2

    def home(c, carry):
        for j in range(blocks // 2):
            start = pl.multiple_of((c * (blocks // 2) + j) * width, width)
            tile = slab_ref[:, pl.ds(start, width)].astype(F32)
            turned = pltpu.roll(tile, width // 2, 1)
            out_ref[c, 2 * j] = jnp.where(low, tile, turned).astype(BF16)
            out_ref[c, 2 * j + 1] = jnp.where(low, turned, tile).astype(BF16)
        out_ref[c, blocks] = jnp.zeros((states, width), BF16)
        return carry

    lax.fori_loop(0, columns, home, 0)


def pack_kernel(table_ref, doubled_ref, out_ref):
    columns, homes, states, width = out_ref.shape
    low = lax.broadcasted_iota(jnp.int32, (states, width), 1) < width // 2

    def home(c, carry):
        for o in range(columns):
            left = doubled_ref[c, table_ref[c, 2 * o]]
            right = doubled_ref[c, table_ref[c, 2 * o + 1]]
            out_ref[o, c] = jnp.where(low, left, right)
        return carry

    lax.fori_loop(0, homes, home, 0)


def owner_kernel(slab_ref, weights_ref, ham_hbm, margin_hbm, out_ref, ham_ref, margin_ref, density_ref, sems):
    chunks, homes, states, width = slab_ref.shape
    half = width // 2
    copy_ham = pltpu.make_async_copy(ham_hbm, ham_ref, sems.at[0])
    copy_margin = pltpu.make_async_copy(margin_hbm, margin_ref, sems.at[1])
    copy_ham.start()
    copy_margin.start()
    for c in range(homes):
        pair = slab_ref[:, c].reshape(chunks * states, width)
        density_ref[c] = jnp.dot(weights_ref[...], pair, preferred_element_type=F32).astype(BF16)
    copy_ham.wait()
    copy_margin.wait()
    row = lax.broadcasted_iota(jnp.int32, (half, width), 0)
    lane = lax.broadcasted_iota(jnp.int32, (half, width), 1)
    masks = [lane == row + half * k for k in range(2)]
    for c in range(homes):
        change = jnp.concatenate(
            [ham_ref[2 * c : 2 * c + 2].reshape(6 * half, width), margin_ref[2 * c : 2 * c + 2].reshape(6 * half, width)],
            axis=1,
        )
        product = jnp.dot(change, density_ref[c], preferred_element_type=F32)
        product = product.reshape(2, 3, half, width)
        parts = []
        for x in range(3):
            kept = jnp.where(masks[0], product[0, x], 0.0) + jnp.where(masks[1], product[1, x], 0.0)
            parts.append(jnp.sum(kept, axis=0, keepdims=True))
        force = jnp.concatenate(parts + [jnp.zeros((5, width), F32)], axis=0)
        high = force.astype(BF16)
        low = (force - high.astype(F32)).astype(BF16)
        out_ref[c] = jnp.concatenate([high.astype(F32), low.astype(F32)], axis=0).astype(BF16)


def hot_kernel(owner_ref, atom_ref, out_ref, rows_ref):
    columns, width, atoms = out_ref.shape
    blocks = owner_ref.shape[0]
    half = width // 2
    lane = lax.broadcasted_iota(jnp.int32, (1, width), 1)
    rows_ref[...] = jnp.full(rows_ref.shape, -1, jnp.int32)
    for b in range(blocks):
        o = owner_ref[b]
        rank = jnp.int32(0)
        for earlier in range(b):
            rank = rank + (owner_ref[earlier] == o).astype(jnp.int32)

        @pl.when(o >= 0)
        def _():
            here = rows_ref[pl.ds(o, 1), :]
            rows_ref[pl.ds(o, 1), :] = jnp.where(lane // half == rank, atom_ref[b : b + 1, :], here)

    atom = lax.broadcasted_iota(jnp.int32, (atoms, width), 0)
    for o in range(columns):
        hot = (atom == rows_ref[o : o + 1, :]).astype(F32)
        out_ref[o] = hot.T.astype(BF16)


def gather_kernel(force_ref, hot_ref, out_ref):
    columns = force_ref.shape[0]
    total = jnp.zeros((force_ref.shape[1], hot_ref.shape[2]), F32)
    for o in range(columns):
        total = total + jnp.dot(force_ref[o], hot_ref[o], preferred_element_type=F32)
    out_ref[...] = 2.0 * (total[0:3, : out_ref.shape[1]] + total[8:11, : out_ref.shape[1]])


def per_device(
    eigvec_slab, occupations, energies, tile_owner, margin_change, hamiltonian_change, basis_atom
):
    columns = lax.axis_size("col")
    rows = lax.axis_size("row")
    col_index = lax.axis_index("col")
    row_index = lax.axis_index("row")
    states = eigvec_slab.shape[0]
    blocks = tile_owner.shape[0]
    block_rows = margin_change.shape[2]
    width = margin_change.shape[3]

    def swap(x):
        return lax.all_to_all(x, "col", split_axis=0, concat_axis=0, tiled=True)

    announced = pl.pallas_call(
        announce_kernel,
        grid=(1,),
        in_specs=[whole(SMEM), pl.BlockSpec((states, width), lambda i: (0, 0))],
        out_specs=pl.BlockSpec((columns, states + 16, width), lambda i: (0, 0, 0)),
        out_shape=jax.ShapeDtypeStruct((columns, states + 16, width), BF16),
    )(tile_owner, eigvec_slab)
    heard = swap(announced)
    doubled = pl.pallas_call(
        double_kernel,
        in_specs=[whole()],
        out_specs=whole(),
        out_shape=jax.ShapeDtypeStruct((columns, blocks + 1, states, width), BF16),
        cost_estimate=pl.CostEstimate(flops=4 << 20, bytes_accessed=3 << 20, transcendentals=0),
        compiler_params=pltpu.CompilerParams(vmem_limit_bytes=16 << 20),
    )(eigvec_slab)

    table = heard[:, states, : 2 * columns].astype(jnp.int32)
    packed = pl.pallas_call(
        pack_kernel,
        in_specs=[whole(SMEM), whole()],
        out_specs=whole(),
        out_shape=jax.ShapeDtypeStruct((columns, columns, states, width), BF16),
        compiler_params=pltpu.CompilerParams(vmem_limit_bytes=16 << 20),
    )(table, doubled)
    slabs = swap(packed)

    panel = heard[:, :states, :]
    panel = jnp.where(row_index == 0, panel, jnp.zeros_like(panel))
    reach = 1
    while reach < rows:
        panel = panel + lax.ppermute(panel, "row", [(i, i + reach) for i in range(reach)])
        reach *= 2
    occ = occupations.astype(F32)
    eweight = occ * energies
    panel_t = panel.reshape(columns * states, width).T.astype(F32)
    weights = jnp.concatenate(
        [(panel_t * occ[None, :]).astype(BF16), (panel_t * -eweight[None, :]).astype(BF16)], axis=0
    )

    device = row_index * columns + col_index
    atom = lax.dynamic_slice_in_dim(basis_atom, device * blocks * block_rows, blocks * block_rows)
    atom = (atom - device * ATOMS_DEV).reshape(blocks, block_rows)
    atom = jnp.concatenate([atom, atom], axis=1)
    atoms_padded = -(-ATOMS_DEV // 128) * 128
    hot = pl.pallas_call(
        hot_kernel,
        in_specs=[whole(SMEM), whole()],
        out_specs=whole(),
        out_shape=jax.ShapeDtypeStruct((columns, width, atoms_padded), BF16),
        scratch_shapes=[pltpu.VMEM((columns, width), jnp.int32)],
        cost_estimate=pl.CostEstimate(flops=4 << 20, bytes_accessed=1 << 20, transcendentals=0),
    )(tile_owner, atom)

    force = pl.pallas_call(
        owner_kernel,
        in_specs=[whole(), whole(), whole(pl.ANY), whole(pl.ANY)],
        out_specs=whole(),
        out_shape=jax.ShapeDtypeStruct((columns, 16, width), BF16),
        scratch_shapes=[
            pltpu.VMEM(hamiltonian_change.shape, BF16),
            pltpu.VMEM(margin_change.shape, BF16),
            pltpu.VMEM((columns, 2 * width, width), BF16),
            pltpu.SemaphoreType.DMA((2,)),
        ],
        compiler_params=pltpu.CompilerParams(vmem_limit_bytes=32 << 20),
    )(slabs, weights, hamiltonian_change, margin_change)

    returned = swap(force)
    return pl.pallas_call(
        gather_kernel,
        in_specs=[whole(), whole()],
        out_specs=whole(),
        out_shape=jax.ShapeDtypeStruct((3, ATOMS_DEV), F32),
    )(returned, hot)


def solution(mesh):
    return jax.shard_map(
        per_device,
        mesh=mesh,
        in_specs=(
            P("col", "row"),
            P(),
            P(),
            P(("row", "col")),
            P(("row", "col"), None, None, None),
            P(("row", "col"), None, None, None),
            P(),
        ),
        out_specs=P(None, ("row", "col")),
        check_vma=False,
    )
```

```python
import jax
import jax.numpy as jnp
from jax import lax
from jax.experimental import pallas as pl
from jax.experimental.pallas import tpu as pltpu
from jax.sharding import PartitionSpec as P

ATOMS_DEV = 160
BF16 = jnp.bfloat16
F32 = jnp.float32
VMEM = pltpu.VMEM
SMEM = pltpu.SMEM


def whole(space=VMEM):
    return pl.BlockSpec(memory_space=space)


def slots_of(owner_ref, columns, blocks, shape):
    lane = lax.broadcasted_iota(jnp.int32, shape, 1)
    owner, rank = lane // 2, lane % 2
    first = jnp.full(shape, blocks, jnp.int32)
    last = jnp.full(shape, -1, jnp.int32)
    for b in range(blocks):
        last = jnp.where(owner == owner_ref[b], b, last)
        first = jnp.where(owner == owner_ref[blocks - 1 - b], blocks - 1 - b, first)
    second = jnp.where(last > first, last, blocks)
    return jnp.where(rank == 0, first, second)


def announce_kernel(owner_ref, slab_hbm, out_hbm, own_ref, tile_ref, sems):
    columns, states, width = tile_ref.shape[0], own_ref.shape[0], tile_ref.shape[2]
    blocks = owner_ref.shape[0]
    half = width // 2
    mine = lax.axis_index("col") * (blocks * half)
    own = pltpu.make_async_copy(slab_hbm.at[:, pl.ds(pl.multiple_of(mine, width), blocks * half)], own_ref, sems.at[columns])
    own.start()
    panels = []
    for o in range(columns):
        panels.append(pltpu.make_async_copy(slab_hbm.at[:, pl.ds(0, width)], out_hbm.at[o, pl.ds(0, states), :], sems.at[o]))
        panels[-1].start()
    rows = tile_ref.shape[1]
    table = slots_of(owner_ref, columns, blocks, (rows - states, width))
    tile_ref[:, states:, :] = jnp.broadcast_to(table.astype(F32).astype(BF16)[None], (columns, rows - states, width))
    tile_ref[:, :states, :] = jnp.zeros((columns, states, width), BF16)
    low = lax.broadcasted_iota(jnp.int32, (states, width), 1) < half
    own.wait()
    for b in range(blocks):
        o = owner_ref[b]
        rank = jnp.int32(0)
        for earlier in range(b):
            rank = rank + (owner_ref[earlier] == o).astype(jnp.int32)
        tile = own_ref[:, (b // 2) * width : (b // 2 + 1) * width].astype(F32)
        turned = pltpu.roll(tile, half, 1)
        block = jnp.where(low == (b % 2 == 0), tile, turned).astype(BF16)

        @pl.when(o >= 0)
        def _():
            tile_ref[o, :states, :] = jnp.where(low == (rank == 0), block, tile_ref[o, :states, :])

    rest = pltpu.make_async_copy(tile_ref, out_hbm.at[:, pl.ds(states, rows), :], sems.at[columns + 1])
    rest.start()
    for copy in panels:
        copy.wait()
    rest.wait()


def double_kernel(slab_ref, out_ref):
    columns, blocks, states, width = out_ref.shape
    blocks -= 1
    low = lax.broadcasted_iota(jnp.int32, (states, width), 1) < width // 2

    def home(c, carry):
        for j in range(blocks // 2):
            start = pl.multiple_of((c * (blocks // 2) + j) * width, width)
            tile = slab_ref[:, pl.ds(start, width)].astype(F32)
            turned = pltpu.roll(tile, width // 2, 1)
            out_ref[c, 2 * j] = jnp.where(low, tile, turned).astype(BF16)
            out_ref[c, 2 * j + 1] = jnp.where(low, turned, tile).astype(BF16)
        out_ref[c, blocks] = jnp.zeros((states, width), BF16)
        return carry

    lax.fori_loop(0, columns, home, 0)


def pack_kernel(table_ref, doubled_ref, out_hbm, out_ref, sems):
    columns, homes, states, width = out_ref.shape
    me = lax.axis_index("col")
    low = lax.broadcasted_iota(jnp.int32, (states, width), 1) < width // 2
    copies = [pltpu.make_async_copy(out_ref.at[o], out_hbm.at[o], sems.at[o]) for o in range(columns)]
    for o in range(columns):
        for j in range(homes):
            c = j + (j >= me).astype(jnp.int32)
            left = doubled_ref[c, table_ref[c, 2 * o]]
            right = doubled_ref[c, table_ref[c, 2 * o + 1]]
            out_ref[o, j] = jnp.where(low, left, right)
        copies[o].start()
    for copy in copies:
        copy.wait()


def owner_kernel(slab_ref, heard_ref, weights_ref, ham_hbm, margin_hbm, out_ref, ham_ref, margin_ref, density_ref, sems):
    chunks, _, states, width = slab_ref.shape
    homes = chunks
    half = width // 2
    parts = sems.shape[0]
    share = 2 * homes // parts
    copies = []
    for p in range(parts):
        here = pl.ds(p * share, share)
        copies.append(
            [
                pltpu.make_async_copy(ham_hbm.at[here], ham_ref.at[here], sems.at[p, 0]),
                pltpu.make_async_copy(margin_hbm.at[here], margin_ref.at[here], sems.at[p, 1]),
            ]
        )
        for copy in copies[p]:
            copy.start()

    def pair_of(c):
        pieces = []
        for d in range(chunks):
            pieces.append(heard_ref[c, states : 2 * states, :] if d == c else slab_ref[d, c - (c > d)])
        return jnp.concatenate(pieces, axis=0)

    for c in range(0, homes, 2):
        two = jnp.concatenate([pair_of(c), pair_of(c + 1)], axis=1)
        density = jnp.dot(weights_ref[...], two, preferred_element_type=F32).astype(BF16)
        density_ref[:, c * width : (c + 2) * width] = density
    row = lax.broadcasted_iota(jnp.int32, (half, width), 0)
    lane = lax.broadcasted_iota(jnp.int32, (half, width), 1)
    masks = [lane == row + half * k for k in range(2)]
    slim = lax.broadcasted_iota(jnp.int32, (8, width), 0)
    for c in range(homes):
        if 2 * c % share == 0:
            for copy in copies[2 * c // share]:
                copy.wait()
        change = jnp.concatenate(
            [ham_ref[2 * c : 2 * c + 2].reshape(6 * half, width), margin_ref[2 * c : 2 * c + 2].reshape(6 * half, width)],
            axis=1,
        )
        product = jnp.dot(change, density_ref[:, c * width : (c + 1) * width], preferred_element_type=F32)
        product = product.reshape(2, 3, half, width)
        force = jnp.zeros((8, width), F32)
        for x in range(3):
            kept = jnp.where(masks[0], product[0, x], 0.0) + jnp.where(masks[1], product[1, x], 0.0)
            force = jnp.where(slim == x, jnp.sum(kept, axis=0, keepdims=True), force)
        high = force.astype(BF16).astype(F32)
        out_ref[c] = jnp.concatenate([high, force - high], axis=0).astype(BF16)


def hot_kernel(owner_ref, atom_ref, out_ref, rows_ref):
    columns, width, atoms = out_ref.shape
    blocks = owner_ref.shape[0]
    half = width // 2
    lane = lax.broadcasted_iota(jnp.int32, (1, width), 1)
    rows_ref[...] = jnp.full(rows_ref.shape, -1, jnp.int32)
    for b in range(blocks):
        o = owner_ref[b]
        rank = jnp.int32(0)
        for earlier in range(b):
            rank = rank + (owner_ref[earlier] == o).astype(jnp.int32)

        @pl.when(o >= 0)
        def _():
            here = rows_ref[pl.ds(o, 1), :]
            rows_ref[pl.ds(o, 1), :] = jnp.where(lane // half == rank, atom_ref[b : b + 1, :], here)

    atom = lax.broadcasted_iota(jnp.int32, (atoms, width), 0)
    for o in range(columns):
        hot = (atom == rows_ref[o : o + 1, :]).astype(F32)
        out_ref[o] = hot.T.astype(BF16)


def gather_kernel(force_ref, hot_ref, out_ref):
    columns = force_ref.shape[0]
    total = jnp.zeros((force_ref.shape[1], hot_ref.shape[2]), F32)
    for o in range(columns):
        total = total + jnp.dot(force_ref[o], hot_ref[o], preferred_element_type=F32)
    out_ref[...] = 2.0 * (total[0:3, : out_ref.shape[1]] + total[8:11, : out_ref.shape[1]])


def per_device(
    eigvec_slab, occupations, energies, tile_owner, margin_change, hamiltonian_change, basis_atom
):
    columns = lax.axis_size("col")
    rows = lax.axis_size("row")
    col_index = lax.axis_index("col")
    row_index = lax.axis_index("row")
    states = eigvec_slab.shape[0]
    blocks = tile_owner.shape[0]
    block_rows = margin_change.shape[2]
    width = margin_change.shape[3]

    def swap(x):
        return lax.all_to_all(x, "col", split_axis=0, concat_axis=0, tiled=True)

    rows_heard = 2 * states + 16
    announced = pl.pallas_call(
        announce_kernel,
        in_specs=[whole(SMEM), whole(pltpu.HBM)],
        out_specs=whole(pltpu.HBM),
        out_shape=jax.ShapeDtypeStruct((columns, rows_heard, width), BF16),
        scratch_shapes=[
            pltpu.VMEM((states, blocks * block_rows), BF16),
            pltpu.VMEM((columns, states + 16, width), BF16),
            pltpu.SemaphoreType.DMA((columns + 2,)),
        ],
        compiler_params=pltpu.CompilerParams(vmem_limit_bytes=4 << 20),
    )(tile_owner, eigvec_slab)
    heard = swap(announced)
    doubled = pl.pallas_call(
        double_kernel,
        in_specs=[whole()],
        out_specs=whole(),
        out_shape=jax.ShapeDtypeStruct((columns, blocks + 1, states, width), BF16),
        cost_estimate=pl.CostEstimate(flops=4 << 20, bytes_accessed=3 << 20, transcendentals=0),
        compiler_params=pltpu.CompilerParams(vmem_limit_bytes=16 << 20),
    )(eigvec_slab)

    table = heard[:, 2 * states, : 2 * columns].astype(jnp.int32)
    packed_shape = (columns, columns - 1, states, width)
    packed = pl.pallas_call(
        pack_kernel,
        in_specs=[whole(SMEM), whole()],
        out_specs=whole(pltpu.HBM),
        out_shape=jax.ShapeDtypeStruct(packed_shape, BF16),
        scratch_shapes=[pltpu.VMEM(packed_shape, BF16), pltpu.SemaphoreType.DMA((columns,))],
        compiler_params=pltpu.CompilerParams(vmem_limit_bytes=16 << 20),
    )(table, doubled)
    slabs = swap(packed)

    panel = heard[:, :states, :]
    panel = jnp.where(row_index == 0, panel, jnp.zeros_like(panel))
    reach = 1
    while reach < rows:
        panel = panel + lax.ppermute(panel, "row", [(i, i + reach) for i in range(reach)])
        reach *= 2
    occ = occupations.astype(F32)
    eweight = occ * energies
    panel_t = panel.reshape(columns * states, width).T.astype(F32)
    weights = jnp.concatenate(
        [(panel_t * occ[None, :]).astype(BF16), (panel_t * -eweight[None, :]).astype(BF16)], axis=0
    )

    device = row_index * columns + col_index
    atom = lax.dynamic_slice_in_dim(basis_atom, device * blocks * block_rows, blocks * block_rows)
    atom = (atom - device * ATOMS_DEV).reshape(blocks, block_rows)
    atom = jnp.concatenate([atom, atom], axis=1)
    atoms_padded = -(-ATOMS_DEV // 128) * 128
    hot = pl.pallas_call(
        hot_kernel,
        in_specs=[whole(SMEM), whole()],
        out_specs=whole(),
        out_shape=jax.ShapeDtypeStruct((columns, width, atoms_padded), BF16),
        scratch_shapes=[pltpu.VMEM((columns, width), jnp.int32)],
        cost_estimate=pl.CostEstimate(flops=4 << 20, bytes_accessed=1 << 20, transcendentals=0),
        compiler_params=pltpu.CompilerParams(vmem_limit_bytes=8 << 20),
    )(tile_owner, atom)

    force = pl.pallas_call(
        owner_kernel,
        in_specs=[whole(), whole(), whole(), whole(pltpu.HBM), whole(pltpu.HBM)],
        out_specs=whole(),
        out_shape=jax.ShapeDtypeStruct((columns, 16, width), BF16),
        scratch_shapes=[
            pltpu.VMEM(hamiltonian_change.shape, BF16),
            pltpu.VMEM(margin_change.shape, BF16),
            pltpu.VMEM((2 * width, columns * width), BF16),
            pltpu.SemaphoreType.DMA((4, 2)),
        ],
        compiler_params=pltpu.CompilerParams(vmem_limit_bytes=32 << 20),
    )(slabs, heard, weights, hamiltonian_change, margin_change)

    returned = swap(force)
    return pl.pallas_call(
        gather_kernel,
        in_specs=[whole(), whole()],
        out_specs=whole(),
        out_shape=jax.ShapeDtypeStruct((3, ATOMS_DEV), F32),
        compiler_params=pltpu.CompilerParams(vmem_limit_bytes=8 << 20),
    )(returned, hot)


def solution(mesh):
    return jax.shard_map(
        per_device,
        mesh=mesh,
        in_specs=(
            P("col", "row"),
            P(),
            P(),
            P(("row", "col")),
            P(("row", "col"), None, None, None),
            P(("row", "col"), None, None, None),
            P(),
        ),
        out_specs=P(None, ("row", "col")),
        check_vma=False,
    )
```

```python
import jax
import jax.numpy as jnp
from jax import lax
from jax.experimental import pallas as pl
from jax.experimental.pallas import tpu as pltpu
from jax.sharding import PartitionSpec as P

ATOMS_DEV = 160
BF16 = jnp.bfloat16
F32 = jnp.float32
VMEM = pltpu.VMEM
SMEM = pltpu.SMEM


def whole(space=VMEM):
    return pl.BlockSpec(memory_space=space)


def slots_of(owner_ref, columns, blocks, shape):
    lane = lax.broadcasted_iota(jnp.int32, shape, 1)
    owner, rank = lane // 2, lane % 2
    first = jnp.full(shape, blocks, jnp.int32)
    last = jnp.full(shape, -1, jnp.int32)
    for b in range(blocks):
        last = jnp.where(owner == owner_ref[b], b, last)
        first = jnp.where(owner == owner_ref[blocks - 1 - b], blocks - 1 - b, first)
    second = jnp.where(last > first, last, blocks)
    return jnp.where(rank == 0, first, second)


def announce_kernel(owner_ref, panel_ref, out_ref):
    columns, _, width = out_ref.shape
    states = panel_ref.shape[0]
    out_ref[:, :states, :] = jnp.broadcast_to(panel_ref[...][None], (columns, states, width))
    table = slots_of(owner_ref, columns, owner_ref.shape[0], (16, width))
    out_ref[:, states:, :] = jnp.broadcast_to(table.astype(F32).astype(BF16)[None], (columns, 16, width))


def double_kernel(slab_ref, out_ref):
    columns, blocks, states, width = out_ref.shape
    blocks -= 1
    low = lax.broadcasted_iota(jnp.int32, (states, width), 1) < width // 2

    def home(c, carry):
        for j in range(blocks // 2):
            start = pl.multiple_of((c * (blocks // 2) + j) * width, width)
            tile = slab_ref[:, pl.ds(start, width)].astype(F32)
            turned = pltpu.roll(tile, width // 2, 1)
            out_ref[c, 2 * j] = jnp.where(low, tile, turned).astype(BF16)
            out_ref[c, 2 * j + 1] = jnp.where(low, turned, tile).astype(BF16)
        out_ref[c, blocks] = jnp.zeros((states, width), BF16)
        return carry

    lax.fori_loop(0, columns, home, 0)


def pack_kernel(table_ref, doubled_ref, out_ref):
    columns, homes, states, width = out_ref.shape
    low = lax.broadcasted_iota(jnp.int32, (states, width), 1) < width // 2

    def home(c, carry):
        for o in range(columns):
            left = doubled_ref[c, table_ref[c, 2 * o]]
            right = doubled_ref[c, table_ref[c, 2 * o + 1]]
            out_ref[o, c] = jnp.where(low, left, right)
        return carry

    lax.fori_loop(0, homes, home, 0)


def change_kernel(ham_ref, margin_ref, out_ref):
    homes, rows, width = out_ref.shape
    for c in range(homes):
        out_ref[c, :, : width // 2] = ham_ref[2 * c : 2 * c + 2].reshape(rows, width // 2)
        out_ref[c, :, width // 2 :] = margin_ref[2 * c : 2 * c + 2].reshape(rows, width // 2)


def owner_kernel(slab_ref, weights_ref, change_ref, out_ref, density_ref):
    chunks, homes, states, width = slab_ref.shape
    half = width // 2
    slabs = jnp.concatenate([slab_ref[:, c].reshape(chunks * states, width) for c in range(homes)], axis=1)
    density_ref[...] = jnp.dot(weights_ref[...], slabs, preferred_element_type=F32).astype(BF16)
    row = lax.broadcasted_iota(jnp.int32, (half, width), 0)
    lane = lax.broadcasted_iota(jnp.int32, (half, width), 1)
    masks = [lane == row + half * k for k in range(2)]
    slim = lax.broadcasted_iota(jnp.int32, (8, width), 0)
    for c in range(homes):
        product = jnp.dot(change_ref[c], density_ref[:, c * width : (c + 1) * width], preferred_element_type=F32)
        product = product.reshape(2, 3, half, width)
        force = jnp.zeros((8, width), F32)
        for x in range(3):
            kept = jnp.where(masks[0], product[0, x], 0.0) + jnp.where(masks[1], product[1, x], 0.0)
            force = jnp.where(slim == x, jnp.sum(kept, axis=0, keepdims=True), force)
        high = force.astype(BF16).astype(F32)
        out_ref[c] = jnp.concatenate([high, force - high], axis=0).astype(BF16)


def hot_kernel(owner_ref, atom_ref, out_ref, rows_ref):
    columns, width, atoms = out_ref.shape
    blocks = owner_ref.shape[0]
    half = width // 2
    lane = lax.broadcasted_iota(jnp.int32, (1, width), 1)
    rows_ref[...] = jnp.full(rows_ref.shape, -1, jnp.int32)
    for b in range(blocks):
        o = owner_ref[b]
        rank = jnp.int32(0)
        for earlier in range(b):
            rank = rank + (owner_ref[earlier] == o).astype(jnp.int32)

        @pl.when(o >= 0)
        def _():
            here = rows_ref[pl.ds(o, 1), :]
            rows_ref[pl.ds(o, 1), :] = jnp.where(lane // half == rank, atom_ref[b : b + 1, :], here)

    atom = lax.broadcasted_iota(jnp.int32, (atoms, width), 0)
    for o in range(columns):
        hot = (atom == rows_ref[o : o + 1, :]).astype(F32)
        out_ref[o] = hot.T.astype(BF16)


def gather_kernel(force_ref, hot_ref, out_ref):
    columns = force_ref.shape[0]
    total = jnp.zeros((force_ref.shape[1], hot_ref.shape[2]), F32)
    for o in range(columns):
        total = total + jnp.dot(force_ref[o], hot_ref[o], preferred_element_type=F32)
    out_ref[...] = 2.0 * (total[0:3, : out_ref.shape[1]] + total[8:11, : out_ref.shape[1]])


def per_device(
    eigvec_slab, occupations, energies, tile_owner, margin_change, hamiltonian_change, basis_atom
):
    columns = lax.axis_size("col")
    rows = lax.axis_size("row")
    col_index = lax.axis_index("col")
    row_index = lax.axis_index("row")
    states = eigvec_slab.shape[0]
    blocks = tile_owner.shape[0]
    block_rows = margin_change.shape[2]
    width = margin_change.shape[3]

    def swap(x):
        return lax.all_to_all(x, "col", split_axis=0, concat_axis=0, tiled=True)

    announced = pl.pallas_call(
        announce_kernel,
        grid=(1,),
        in_specs=[whole(SMEM), pl.BlockSpec((states, width), lambda i: (0, 0))],
        out_specs=pl.BlockSpec((columns, states + 16, width), lambda i: (0, 0, 0)),
        out_shape=jax.ShapeDtypeStruct((columns, states + 16, width), BF16),
    )(tile_owner, eigvec_slab)
    heard = swap(announced)
    doubled = pl.pallas_call(
        double_kernel,
        in_specs=[whole()],
        out_specs=whole(),
        out_shape=jax.ShapeDtypeStruct((columns, blocks + 1, states, width), BF16),
        cost_estimate=pl.CostEstimate(flops=4 << 20, bytes_accessed=3 << 20, transcendentals=0),
        compiler_params=pltpu.CompilerParams(vmem_limit_bytes=16 << 20),
    )(eigvec_slab)

    table = heard[:, states, : 2 * columns].astype(jnp.int32)
    packed = pl.pallas_call(
        pack_kernel,
        in_specs=[whole(SMEM), whole()],
        out_specs=whole(),
        out_shape=jax.ShapeDtypeStruct((columns, columns, states, width), BF16),
        compiler_params=pltpu.CompilerParams(vmem_limit_bytes=16 << 20),
    )(table, doubled)
    slabs = swap(packed)

    panel = heard[:, :states, :]
    panel = jnp.where(row_index == 0, panel, jnp.zeros_like(panel))
    reach = 1
    while reach < rows:
        panel = panel + lax.ppermute(panel, "row", [(i, i + reach) for i in range(reach)])
        reach *= 2
    occ = occupations.astype(F32)
    eweight = occ * energies
    panel_t = panel.reshape(columns * states, width).T.astype(F32)
    weights = jnp.concatenate(
        [(panel_t * occ[None, :]).astype(BF16), (panel_t * -eweight[None, :]).astype(BF16)], axis=0
    )

    weights, ham, margin, owner = lax.optimization_barrier(
        (weights, hamiltonian_change, margin_change, tile_owner)
    )

    device = row_index * columns + col_index
    atom = lax.dynamic_slice_in_dim(basis_atom, device * blocks * block_rows, blocks * block_rows)
    atom = (atom - device * ATOMS_DEV).reshape(blocks, block_rows)
    atom = jnp.concatenate([atom, atom], axis=1)
    atoms_padded = -(-ATOMS_DEV // 128) * 128
    hot = pl.pallas_call(
        hot_kernel,
        in_specs=[whole(SMEM), whole()],
        out_specs=whole(),
        out_shape=jax.ShapeDtypeStruct((columns, width, atoms_padded), BF16),
        scratch_shapes=[pltpu.VMEM((columns, width), jnp.int32)],
        cost_estimate=pl.CostEstimate(flops=4 << 20, bytes_accessed=1 << 20, transcendentals=0),
        compiler_params=pltpu.CompilerParams(vmem_limit_bytes=8 << 20),
    )(owner, atom)

    change = pl.pallas_call(
        change_kernel,
        in_specs=[whole(), whole()],
        out_specs=whole(),
        out_shape=jax.ShapeDtypeStruct((columns, 6 * block_rows, 2 * width), BF16),
        cost_estimate=pl.CostEstimate(flops=1 << 20, bytes_accessed=6 << 20, transcendentals=0),
        compiler_params=pltpu.CompilerParams(vmem_limit_bytes=16 << 20),
    )(ham, margin)
    slabs, weights, change, hot = lax.optimization_barrier((slabs, weights, change, hot))
    force = pl.pallas_call(
        owner_kernel,
        in_specs=[whole(), whole(), whole()],
        out_specs=whole(),
        out_shape=jax.ShapeDtypeStruct((columns, 16, width), BF16),
        scratch_shapes=[pltpu.VMEM((2 * width, columns * width), BF16)],
        compiler_params=pltpu.CompilerParams(vmem_limit_bytes=16 << 20),
    )(slabs, weights, change)

    returned = swap(force)
    return pl.pallas_call(
        gather_kernel,
        in_specs=[whole(), whole()],
        out_specs=whole(),
        out_shape=jax.ShapeDtypeStruct((3, ATOMS_DEV), F32),
        compiler_params=pltpu.CompilerParams(vmem_limit_bytes=8 << 20),
    )(returned, hot)


def solution(mesh):
    return jax.shard_map(
        per_device,
        mesh=mesh,
        in_specs=(
            P("col", "row"),
            P(),
            P(),
            P(("row", "col")),
            P(("row", "col"), None, None, None),
            P(("row", "col"), None, None, None),
            P(),
        ),
        out_specs=P(None, ("row", "col")),
        check_vma=False,
    )
```

```python
import jax
import jax.numpy as jnp
from jax import lax
from jax.experimental import pallas as pl
from jax.experimental.pallas import tpu as pltpu
from jax.sharding import PartitionSpec as P

ATOMS_DEV = 160
ORDER = (0, 1, 2, 3, 4, 5, 6, 7, 8, 9, 10, 11, 12, 13, 14, 15)
FIRST = (7, 8, 6, 14, 1, 3, 9, 12, 13, 0, 4, 11, 5, 10, 2, 15)
HEARD = tuple(FIRST.index(column) for column in range(len(FIRST)))
BACK = (2, 8, 6, 14, 9, 3, 1, 5, 7, 15, 4, 11, 12, 13, 10, 0)
RETURN = tuple(BACK.index(column) for column in range(len(BACK)))
PLACE = tuple(ORDER.index(column) for column in range(len(ORDER)))
BF16 = jnp.bfloat16
F32 = jnp.float32
VMEM = pltpu.VMEM
SMEM = pltpu.SMEM


def whole(space=VMEM):
    return pl.BlockSpec(memory_space=space)


def slots_of(owner_ref, columns, blocks, shape):
    lane = lax.broadcasted_iota(jnp.int32, shape, 1)
    owner, rank = lane // 2, lane % 2
    first = jnp.full(shape, blocks, jnp.int32)
    last = jnp.full(shape, -1, jnp.int32)
    for b in range(blocks):
        last = jnp.where(owner == owner_ref[b], b, last)
        first = jnp.where(owner == owner_ref[blocks - 1 - b], blocks - 1 - b, first)
    second = jnp.where(last > first, last, blocks)
    return jnp.where(rank == 0, first, second)


def announce_kernel(owner_ref, panel_ref, out_ref):
    columns, _, width = out_ref.shape
    states = panel_ref.shape[0]
    out_ref[:, :states, :] = jnp.broadcast_to(panel_ref[...][None], (columns, states, width))
    table = slots_of(owner_ref, columns, owner_ref.shape[0], (16, width))
    out_ref[:, states:, :] = jnp.broadcast_to(table.astype(F32).astype(BF16)[None], (columns, 16, width))


def double_kernel(slab_ref, out_ref):
    columns, blocks, states, width = out_ref.shape
    blocks -= 1
    low = lax.broadcasted_iota(jnp.int32, (states, width), 1) < width // 2
    for place in range(columns):
        for j in range(blocks // 2):
            start = (FIRST[place] * (blocks // 2) + j) * width
            tile = slab_ref[:, start : start + width].astype(F32)
            turned = pltpu.roll(tile, width // 2, 1)
            out_ref[place, 2 * j] = jnp.where(low, tile, turned).astype(BF16)
            out_ref[place, 2 * j + 1] = jnp.where(low, turned, tile).astype(BF16)
        out_ref[place, blocks] = jnp.zeros((states, width), BF16)


def pack_kernel(table_ref, doubled_ref, out_ref):
    columns, homes, states, width = out_ref.shape
    low = lax.broadcasted_iota(jnp.int32, (states, width), 1) < width // 2

    def home(h, carry):
        for o in range(columns):
            left = doubled_ref[h, table_ref[h, 2 * o]]
            right = doubled_ref[h, table_ref[h, 2 * o + 1]]
            out_ref[PLACE[o], h] = jnp.where(low, left, right)
        return carry

    lax.fori_loop(0, homes, home, 0)


def weights_kernel(panel_ref, scale_ref, out_ref):
    columns, states, width = panel_ref.shape
    panel = jnp.concatenate([panel_ref[HEARD[column]] for column in ORDER], axis=0).astype(F32).T
    scale = jnp.concatenate([scale_ref[:, column * states : (column + 1) * states] for column in ORDER], axis=1)
    out_ref[:width, :] = (panel * scale[0:1, :]).astype(BF16)
    out_ref[width:, :] = (panel * scale[1:2, :]).astype(BF16)


def change_kernel(ham_ref, margin_ref, out_ref):
    homes, rows, width = out_ref.shape
    for c in range(homes):
        out_ref[c, :, : width // 2] = ham_ref[2 * c : 2 * c + 2].reshape(rows, width // 2)
        out_ref[c, :, width // 2 :] = margin_ref[2 * c : 2 * c + 2].reshape(rows, width // 2)


def owner_kernel(slab_any, weights_ref, change_ref, out_ref, slab_ref, total_ref, density_ref, sems):
    chunks, homes, states, width = slab_ref.shape
    half = width // 2
    share = chunks // 2
    copies = []
    for p in range(2):
        here = pl.ds(p * share, share)
        copies.append(pltpu.make_async_copy(slab_any.at[here], slab_ref.at[here], sems.at[p]))
        copies[p].start()
    for p in range(2):
        copies[p].wait()
        slabs = jnp.concatenate(
            [slab_ref[p * share : (p + 1) * share, c].reshape(share * states, width) for c in range(homes)], axis=1
        )
        part = jnp.dot(
            weights_ref[:, p * share * states : (p + 1) * share * states], slabs, preferred_element_type=F32
        )
        if p == 0:
            total_ref[...] = part
        else:
            density_ref[...] = (total_ref[...] + part).astype(BF16)
    row = lax.broadcasted_iota(jnp.int32, (half, width), 0)
    lane = lax.broadcasted_iota(jnp.int32, (half, width), 1)
    masks = [lane == row + half * k for k in range(2)]
    slim = lax.broadcasted_iota(jnp.int32, (8, width), 0)
    for h in range(homes):
        c = FIRST[h]
        product = jnp.dot(change_ref[c], density_ref[:, h * width : (h + 1) * width], preferred_element_type=F32)
        product = product.reshape(2, 3, half, width)
        force = jnp.zeros((8, width), F32)
        for x in range(3):
            kept = jnp.where(masks[0], product[0, x], 0.0) + jnp.where(masks[1], product[1, x], 0.0)
            force = jnp.where(slim == x, jnp.sum(kept, axis=0, keepdims=True), force)
        high = force.astype(BF16).astype(F32)
        out_ref[RETURN[c]] = jnp.concatenate([high, force - high], axis=0).astype(BF16)


def hot_kernel(owner_ref, atom_ref, out_ref, rows_ref):
    columns, width, atoms = out_ref.shape
    blocks = owner_ref.shape[0]
    half = width // 2
    lane = lax.broadcasted_iota(jnp.int32, (1, width), 1)
    rows_ref[...] = jnp.full(rows_ref.shape, -1, jnp.int32)
    for b in range(blocks):
        o = owner_ref[b]
        rank = jnp.int32(0)
        for earlier in range(b):
            rank = rank + (owner_ref[earlier] == o).astype(jnp.int32)

        @pl.when(o >= 0)
        def _():
            here = rows_ref[pl.ds(o, 1), :]
            rows_ref[pl.ds(o, 1), :] = jnp.where(lane // half == rank, atom_ref[b : b + 1, :], here)

    atom = lax.broadcasted_iota(jnp.int32, (atoms, width), 0)
    for o in range(columns):
        hot = (atom == rows_ref[o : o + 1, :]).astype(F32)
        out_ref[o] = hot.T.astype(BF16)


def gather_kernel(force_ref, hot_ref, out_ref):
    columns = force_ref.shape[0]
    total = jnp.zeros((force_ref.shape[1], hot_ref.shape[2]), F32)
    for o in range(columns):
        total = total + jnp.dot(force_ref[RETURN[o]], hot_ref[o], preferred_element_type=F32)
    out_ref[...] = 2.0 * (total[0:3, : out_ref.shape[1]] + total[8:11, : out_ref.shape[1]])


def per_device(
    eigvec_slab, occupations, energies, tile_owner, margin_change, hamiltonian_change, basis_atom
):
    columns = lax.axis_size("col")
    rows = lax.axis_size("row")
    col_index = lax.axis_index("col")
    row_index = lax.axis_index("row")
    states = eigvec_slab.shape[0]
    blocks = tile_owner.shape[0]
    block_rows = margin_change.shape[2]
    width = margin_change.shape[3]

    def swap(x, groups=None):
        return lax.all_to_all(x, "col", split_axis=0, concat_axis=0, tiled=True, axis_index_groups=groups)

    announced = pl.pallas_call(
        announce_kernel,
        grid=(1,),
        in_specs=[whole(SMEM), pl.BlockSpec((states, width), lambda i: (0, 0))],
        out_specs=pl.BlockSpec((columns, states + 16, width), lambda i: (0, 0, 0)),
        out_shape=jax.ShapeDtypeStruct((columns, states + 16, width), BF16),
    )(tile_owner, eigvec_slab)
    heard = swap(announced, [list(FIRST)])
    doubled = pl.pallas_call(
        double_kernel,
        in_specs=[whole()],
        out_specs=whole(),
        out_shape=jax.ShapeDtypeStruct((columns, blocks + 1, states, width), BF16),
        cost_estimate=pl.CostEstimate(flops=4 << 20, bytes_accessed=3 << 20, transcendentals=0),
        compiler_params=pltpu.CompilerParams(vmem_limit_bytes=16 << 20),
    )(eigvec_slab)

    table = heard[:, states, : 2 * columns].astype(jnp.int32)
    packed = pl.pallas_call(
        pack_kernel,
        in_specs=[whole(SMEM), whole()],
        out_specs=whole(),
        out_shape=jax.ShapeDtypeStruct((columns, columns, states, width), BF16),
        compiler_params=pltpu.CompilerParams(vmem_limit_bytes=16 << 20),
    )(table, doubled)
    slabs = swap(packed, [list(ORDER)])

    panel = heard[:, :states, :]
    panel = jnp.where(row_index == 0, panel, jnp.zeros_like(panel))
    reach = 1
    while reach < rows:
        panel = panel + lax.ppermute(panel, "row", [(i, i + reach) for i in range(reach)])
        reach *= 2
    occ = occupations.astype(F32)
    eweight = occ * energies
    weights = pl.pallas_call(
        weights_kernel,
        in_specs=[whole(), whole()],
        out_specs=whole(),
        out_shape=jax.ShapeDtypeStruct((2 * width, columns * states), BF16),
        cost_estimate=pl.CostEstimate(flops=1 << 20, bytes_accessed=1 << 19, transcendentals=0),
        compiler_params=pltpu.CompilerParams(vmem_limit_bytes=8 << 20),
    )(panel, jnp.stack([occ, -eweight]))

    weights, ham, margin, owner = lax.optimization_barrier(
        (weights, hamiltonian_change, margin_change, tile_owner)
    )

    device = row_index * columns + col_index
    atom = lax.dynamic_slice_in_dim(basis_atom, device * blocks * block_rows, blocks * block_rows)
    atom = (atom - device * ATOMS_DEV).reshape(blocks, block_rows)
    atom = jnp.concatenate([atom, atom], axis=1)
    atoms_padded = -(-ATOMS_DEV // 128) * 128
    hot = pl.pallas_call(
        hot_kernel,
        in_specs=[whole(SMEM), whole()],
        out_specs=whole(),
        out_shape=jax.ShapeDtypeStruct((columns, width, atoms_padded), BF16),
        scratch_shapes=[pltpu.VMEM((columns, width), jnp.int32)],
        cost_estimate=pl.CostEstimate(flops=4 << 20, bytes_accessed=1 << 20, transcendentals=0),
        compiler_params=pltpu.CompilerParams(vmem_limit_bytes=8 << 20),
    )(owner, atom)

    change = pl.pallas_call(
        change_kernel,
        in_specs=[whole(), whole()],
        out_specs=whole(),
        out_shape=jax.ShapeDtypeStruct((columns, 6 * block_rows, 2 * width), BF16),
        cost_estimate=pl.CostEstimate(flops=1 << 20, bytes_accessed=6 << 20, transcendentals=0),
        compiler_params=pltpu.CompilerParams(vmem_limit_bytes=16 << 20),
    )(ham, margin)
    slabs, weights, change, hot = lax.optimization_barrier((slabs, weights, change, hot))
    force = pl.pallas_call(
        owner_kernel,
        in_specs=[whole(pl.ANY), whole(), whole()],
        out_specs=whole(),
        out_shape=jax.ShapeDtypeStruct((columns, 16, width), BF16),
        scratch_shapes=[
            pltpu.VMEM(slabs.shape, BF16),
            pltpu.VMEM((2 * width, columns * width), F32),
            pltpu.VMEM((2 * width, columns * width), BF16),
            pltpu.SemaphoreType.DMA((2,)),
        ],
        compiler_params=pltpu.CompilerParams(vmem_limit_bytes=16 << 20),
    )(slabs, weights, change)

    returned = swap(force, [list(BACK)])
    return pl.pallas_call(
        gather_kernel,
        in_specs=[whole(), whole()],
        out_specs=whole(),
        out_shape=jax.ShapeDtypeStruct((3, ATOMS_DEV), F32),
        compiler_params=pltpu.CompilerParams(vmem_limit_bytes=8 << 20),
    )(returned, hot)


def solution(mesh):
    return jax.shard_map(
        per_device,
        mesh=mesh,
        in_specs=(
            P("col", "row"),
            P(),
            P(),
            P(("row", "col")),
            P(("row", "col"), None, None, None),
            P(("row", "col"), None, None, None),
            P(),
        ),
        out_specs=P(None, ("row", "col")),
        check_vma=False,
    )
```

```python
import jax
import jax.numpy as jnp
from jax import lax
from jax.experimental import pallas as pl
from jax.experimental.pallas import tpu as pltpu
from jax.sharding import PartitionSpec as P

ATOMS_DEV = 160
FIRST = (7, 9, 6, 14, 1, 3, 8, 12, 15, 0, 4, 11, 5, 10, 2, 13)
BACK = (8, 9, 0, 1, 4, 12, 13, 11, 2, 10, 15, 3, 7, 5, 14, 6)
HEARD = tuple(FIRST.index(column) for column in range(len(FIRST)))
RETURN = tuple(BACK.index(column) for column in range(len(BACK)))
BF16 = jnp.bfloat16
F32 = jnp.float32
VMEM = pltpu.VMEM
SMEM = pltpu.SMEM


def whole(space=VMEM):
    return pl.BlockSpec(memory_space=space)


def slots_of(owner_ref, columns, blocks, shape):
    lane = lax.broadcasted_iota(jnp.int32, shape, 1)
    owner, rank = lane // 2, lane % 2
    first = jnp.full(shape, blocks, jnp.int32)
    last = jnp.full(shape, -1, jnp.int32)
    for b in range(blocks):
        last = jnp.where(owner == owner_ref[b], b, last)
        first = jnp.where(owner == owner_ref[blocks - 1 - b], blocks - 1 - b, first)
    second = jnp.where(last > first, last, blocks)
    return jnp.where(rank == 0, first, second)


def announce_kernel(owner_ref, panel_ref, out_ref):
    columns, _, width = out_ref.shape
    states = panel_ref.shape[0]
    out_ref[:, :states, :] = jnp.broadcast_to(panel_ref[...][None], (columns, states, width))
    table = slots_of(owner_ref, columns, owner_ref.shape[0], (16, width))
    out_ref[:, states:, :] = jnp.broadcast_to(table.astype(F32).astype(BF16)[None], (columns, 16, width))


def pack_kernel(table_ref, slab_ref, out_any, doubled_ref, out_ref, sems):
    columns, homes, states, width = out_ref.shape
    low = lax.broadcasted_iota(jnp.int32, (states, width), 1) < width // 2
    blocks = doubled_ref.shape[1] - 1
    for place in range(homes):
        for j in range(blocks // 2):
            start = (FIRST[place] * (blocks // 2) + j) * width
            tile = slab_ref[:, start : start + width].astype(F32)
            turned = pltpu.roll(tile, width // 2, 1)
            doubled_ref[place, 2 * j] = jnp.where(low, tile, turned).astype(BF16)
            doubled_ref[place, 2 * j + 1] = jnp.where(low, turned, tile).astype(BF16)
        doubled_ref[place, blocks] = jnp.zeros((states, width), BF16)

    def copy(o):
        return pltpu.make_async_copy(out_ref.at[o], out_any.at[o], sems.at[o])

    def column(o, carry):
        for h in range(homes):
            left = doubled_ref[h, table_ref[h, 2 * o]]
            right = doubled_ref[h, table_ref[h, 2 * o + 1]]
            out_ref[o, h] = jnp.where(low, left, right)
        copy(o).start()
        return carry

    def wait(o, carry):
        copy(o).wait()
        return carry

    lax.fori_loop(0, columns, column, 0)
    lax.fori_loop(0, columns, wait, 0)


def weights_kernel(panel_ref, scale_ref, out_ref):
    columns, states, width = panel_ref.shape
    panel = jnp.concatenate([panel_ref[HEARD[column]] for column in range(columns)], axis=0).astype(F32).T
    out_ref[:width, :] = (panel * scale_ref[0:1, :]).astype(BF16)
    out_ref[width:, :] = (panel * scale_ref[1:2, :]).astype(BF16)


def change_kernel(ham_ref, margin_ref, out_ref):
    homes, rows, width = out_ref.shape
    for c in range(homes):
        out_ref[c, :, : width // 2] = ham_ref[2 * c : 2 * c + 2].reshape(rows, width // 2)
        out_ref[c, :, width // 2 :] = margin_ref[2 * c : 2 * c + 2].reshape(rows, width // 2)


def owner_kernel(slab_any, weights_ref, change_ref, out_ref, slab_ref, total_ref, density_ref, sems):
    chunks, homes, states, width = slab_ref.shape
    half = width // 2
    share = chunks // 2
    copies = []
    for p in range(2):
        here = pl.ds(p * share, share)
        copies.append(pltpu.make_async_copy(slab_any.at[here], slab_ref.at[here], sems.at[p]))
        copies[p].start()
    for p in range(2):
        copies[p].wait()
        slabs = jnp.concatenate(
            [slab_ref[p * share : (p + 1) * share, c].reshape(share * states, width) for c in range(homes)], axis=1
        )
        part = jnp.dot(
            weights_ref[:, p * share * states : (p + 1) * share * states], slabs, preferred_element_type=F32
        )
        if p == 0:
            total_ref[...] = part
        else:
            density_ref[...] = (total_ref[...] + part).astype(BF16)
    row = lax.broadcasted_iota(jnp.int32, (half, width), 0)
    lane = lax.broadcasted_iota(jnp.int32, (half, width), 1)
    masks = [lane == row + half * k for k in range(2)]
    slim = lax.broadcasted_iota(jnp.int32, (8, width), 0)
    for h in range(homes):
        c = FIRST[h]
        product = jnp.dot(change_ref[c], density_ref[:, h * width : (h + 1) * width], preferred_element_type=F32)
        product = product.reshape(2, 3, half, width)
        force = jnp.zeros((8, width), F32)
        for x in range(3):
            kept = jnp.where(masks[0], product[0, x], 0.0) + jnp.where(masks[1], product[1, x], 0.0)
            force = jnp.where(slim == x, jnp.sum(kept, axis=0, keepdims=True), force)
        high = force.astype(BF16).astype(F32)
        out_ref[RETURN[c]] = jnp.concatenate([high, force - high], axis=0).astype(BF16)


def hot_kernel(owner_ref, atom_ref, out_ref, rows_ref):
    columns, width, atoms = out_ref.shape
    blocks = owner_ref.shape[0]
    half = width // 2
    lane = lax.broadcasted_iota(jnp.int32, (1, width), 1)
    rows_ref[...] = jnp.full(rows_ref.shape, -1, jnp.int32)
    for b in range(blocks):
        o = owner_ref[b]
        rank = jnp.int32(0)
        for earlier in range(b):
            rank = rank + (owner_ref[earlier] == o).astype(jnp.int32)

        @pl.when(o >= 0)
        def _():
            here = rows_ref[pl.ds(o, 1), :]
            rows_ref[pl.ds(o, 1), :] = jnp.where(lane // half == rank, atom_ref[b : b + 1, :], here)

    atom = lax.broadcasted_iota(jnp.int32, (atoms, width), 0)
    for o in range(columns):
        hot = (atom == rows_ref[o : o + 1, :]).astype(F32)
        out_ref[o] = hot.T.astype(BF16)


def gather_kernel(force_ref, hot_ref, out_ref):
    columns = force_ref.shape[0]
    total = jnp.zeros((force_ref.shape[1], hot_ref.shape[2]), F32)
    for o in range(columns):
        total = total + jnp.dot(force_ref[RETURN[o]], hot_ref[o], preferred_element_type=F32)
    out_ref[...] = 2.0 * (total[0:3, : out_ref.shape[1]] + total[8:11, : out_ref.shape[1]])


def per_device(
    eigvec_slab, occupations, energies, tile_owner, margin_change, hamiltonian_change, basis_atom
):
    columns = lax.axis_size("col")
    rows = lax.axis_size("row")
    col_index = lax.axis_index("col")
    row_index = lax.axis_index("row")
    states = eigvec_slab.shape[0]
    blocks = tile_owner.shape[0]
    block_rows = margin_change.shape[2]
    width = margin_change.shape[3]

    def swap(x, groups=None):
        return lax.all_to_all(x, "col", split_axis=0, concat_axis=0, tiled=True, axis_index_groups=groups)

    announced = pl.pallas_call(
        announce_kernel,
        grid=(1,),
        in_specs=[whole(SMEM), pl.BlockSpec((states, width), lambda i: (0, 0))],
        out_specs=pl.BlockSpec((columns, states + 16, width), lambda i: (0, 0, 0)),
        out_shape=jax.ShapeDtypeStruct((columns, states + 16, width), BF16),
    )(tile_owner, eigvec_slab)
    heard = swap(announced, [list(FIRST)])
    heard, slab = lax.optimization_barrier((heard, eigvec_slab))
    table = heard[:, states, : 2 * columns].astype(jnp.int32)
    packed_shape = (columns, columns, states, width)
    packed = pl.pallas_call(
        pack_kernel,
        in_specs=[whole(SMEM), whole()],
        out_specs=whole(pl.ANY),
        out_shape=jax.ShapeDtypeStruct(packed_shape, BF16),
        scratch_shapes=[
            pltpu.VMEM((columns, blocks + 1, states, width), BF16),
            pltpu.VMEM(packed_shape, BF16),
            pltpu.SemaphoreType.DMA((columns,)),
        ],
        compiler_params=pltpu.CompilerParams(vmem_limit_bytes=16 << 20),
    )(table, slab)
    slabs = swap(packed)

    panel = heard[:, :states, :]
    panel = jnp.where(row_index == 0, panel, jnp.zeros_like(panel))
    reach = 1
    while reach < rows:
        panel = panel + lax.ppermute(panel, "row", [(i, i + reach) for i in range(reach)])
        reach *= 2
    occ = occupations.astype(F32)
    eweight = occ * energies
    weights = pl.pallas_call(
        weights_kernel,
        in_specs=[whole(), whole()],
        out_specs=whole(),
        out_shape=jax.ShapeDtypeStruct((2 * width, columns * states), BF16),
        cost_estimate=pl.CostEstimate(flops=1 << 20, bytes_accessed=1 << 19, transcendentals=0),
        compiler_params=pltpu.CompilerParams(vmem_limit_bytes=8 << 20),
    )(panel, jnp.stack([occ, -eweight]))

    weights, ham, margin, owner = lax.optimization_barrier(
        (weights, hamiltonian_change, margin_change, tile_owner)
    )

    device = row_index * columns + col_index
    atom = lax.dynamic_slice_in_dim(basis_atom, device * blocks * block_rows, blocks * block_rows)
    atom = (atom - device * ATOMS_DEV).reshape(blocks, block_rows)
    atom = jnp.concatenate([atom, atom], axis=1)
    atoms_padded = -(-ATOMS_DEV // 128) * 128
    hot = pl.pallas_call(
        hot_kernel,
        in_specs=[whole(SMEM), whole()],
        out_specs=whole(),
        out_shape=jax.ShapeDtypeStruct((columns, width, atoms_padded), BF16),
        scratch_shapes=[pltpu.VMEM((columns, width), jnp.int32)],
        cost_estimate=pl.CostEstimate(flops=4 << 20, bytes_accessed=1 << 20, transcendentals=0),
        compiler_params=pltpu.CompilerParams(vmem_limit_bytes=8 << 20),
    )(owner, atom)

    change = pl.pallas_call(
        change_kernel,
        in_specs=[whole(), whole()],
        out_specs=whole(),
        out_shape=jax.ShapeDtypeStruct((columns, 6 * block_rows, 2 * width), BF16),
        cost_estimate=pl.CostEstimate(flops=1 << 20, bytes_accessed=6 << 20, transcendentals=0),
        compiler_params=pltpu.CompilerParams(vmem_limit_bytes=16 << 20),
    )(ham, margin)
    slabs, weights, change, hot = lax.optimization_barrier((slabs, weights, change, hot))
    force = pl.pallas_call(
        owner_kernel,
        in_specs=[whole(pl.ANY), whole(), whole()],
        out_specs=whole(),
        out_shape=jax.ShapeDtypeStruct((columns, 16, width), BF16),
        scratch_shapes=[
            pltpu.VMEM(slabs.shape, BF16),
            pltpu.VMEM((2 * width, columns * width), F32),
            pltpu.VMEM((2 * width, columns * width), BF16),
            pltpu.SemaphoreType.DMA((2,)),
        ],
        compiler_params=pltpu.CompilerParams(vmem_limit_bytes=16 << 20),
    )(slabs, weights, change)

    returned = swap(force, [list(BACK)])
    return pl.pallas_call(
        gather_kernel,
        in_specs=[whole(), whole()],
        out_specs=whole(),
        out_shape=jax.ShapeDtypeStruct((3, ATOMS_DEV), F32),
        compiler_params=pltpu.CompilerParams(vmem_limit_bytes=8 << 20),
    )(returned, hot)


def solution(mesh):
    return jax.shard_map(
        per_device,
        mesh=mesh,
        in_specs=(
            P("col", "row"),
            P(),
            P(),
            P(("row", "col")),
            P(("row", "col"), None, None, None),
            P(("row", "col"), None, None, None),
            P(),
        ),
        out_specs=P(None, ("row", "col")),
        check_vma=False,
    )
```

```python
import jax
import jax.numpy as jnp
from jax import lax
from jax.experimental import pallas as pl
from jax.experimental.pallas import tpu as pltpu
from jax.sharding import PartitionSpec as P

ATOMS_DEV = 160
FIRST = (7, 9, 6, 14, 1, 3, 8, 12, 15, 0, 4, 11, 5, 10, 2, 13)
BACK = (8, 9, 0, 1, 4, 12, 13, 11, 2, 10, 15, 3, 7, 5, 14, 6)
HEARD = tuple(FIRST.index(column) for column in range(len(FIRST)))
RETURN = tuple(BACK.index(column) for column in range(len(BACK)))
BF16 = jnp.bfloat16
F32 = jnp.float32
VMEM = pltpu.VMEM
SMEM = pltpu.SMEM


def whole(space=VMEM):
    return pl.BlockSpec(memory_space=space)


def slots_of(owner_ref, columns, blocks, shape):
    lane = lax.broadcasted_iota(jnp.int32, shape, 1)
    owner, rank = lane // 2, lane % 2
    first = jnp.full(shape, blocks, jnp.int32)
    last = jnp.full(shape, -1, jnp.int32)
    for b in range(blocks):
        last = jnp.where(owner == owner_ref[b], b, last)
        first = jnp.where(owner == owner_ref[blocks - 1 - b], blocks - 1 - b, first)
    second = jnp.where(last > first, last, blocks)
    return jnp.where(rank == 0, first, second)


def announce_kernel(owner_ref, panel_ref, out_ref):
    columns, _, width = out_ref.shape
    states = panel_ref.shape[0]
    out_ref[:, :states, :] = jnp.broadcast_to(panel_ref[...][None], (columns, states, width))
    table = slots_of(owner_ref, columns, owner_ref.shape[0], (16, width))
    out_ref[:, states:, :] = jnp.broadcast_to(table.astype(F32).astype(BF16)[None], (columns, 16, width))


def pack_kernel(table_any, slab_ref, out_any, table_ref, doubled_ref, out_ref, sems):
    columns, homes, states, width = out_ref.shape
    low = lax.broadcasted_iota(jnp.int32, (states, width), 1) < width // 2
    blocks = doubled_ref.shape[1] - 1
    table = pltpu.make_async_copy(table_any, table_ref, sems.at[columns])
    table.start()
    for place in range(homes):
        for j in range(blocks // 2):
            start = (FIRST[place] * (blocks // 2) + j) * width
            tile = slab_ref[:, start : start + width].astype(F32)
            turned = pltpu.roll(tile, width // 2, 1)
            doubled_ref[place, 2 * j] = jnp.where(low, tile, turned).astype(BF16)
            doubled_ref[place, 2 * j + 1] = jnp.where(low, turned, tile).astype(BF16)
        doubled_ref[place, blocks] = jnp.zeros((states, width), BF16)

    def copy(o):
        return pltpu.make_async_copy(out_ref.at[o], out_any.at[o], sems.at[o])

    def column(o, carry):
        for h in range(homes):
            left = doubled_ref[h, table_ref[h, 2 * o]]
            right = doubled_ref[h, table_ref[h, 2 * o + 1]]
            out_ref[o, h] = jnp.where(low, left, right)
        copy(o).start()
        return carry

    def wait(o, carry):
        copy(o).wait()
        return carry

    table.wait()
    lax.fori_loop(0, columns, column, 0)
    lax.fori_loop(0, columns, wait, 0)


def weights_kernel(panel_ref, scale_ref, out_ref):
    columns, states, width = panel_ref.shape
    panel = jnp.concatenate([panel_ref[HEARD[column]] for column in range(columns)], axis=0).astype(F32).T
    out_ref[:width, :] = (panel * scale_ref[0:1, :]).astype(BF16)
    out_ref[width:, :] = (panel * scale_ref[1:2, :]).astype(BF16)


def change_kernel(ham_ref, margin_ref, out_ref):
    homes, rows, width = out_ref.shape
    for c in range(homes):
        out_ref[c, :, : width // 2] = ham_ref[2 * c : 2 * c + 2].reshape(rows, width // 2)
        out_ref[c, :, width // 2 :] = margin_ref[2 * c : 2 * c + 2].reshape(rows, width // 2)


def owner_kernel(slab_any, weights_ref, change_ref, out_ref, slab_ref, total_ref, density_ref, sems):
    chunks, homes, states, width = slab_ref.shape
    half = width // 2
    share = chunks // 2
    copies = []
    for p in range(2):
        here = pl.ds(p * share, share)
        copies.append(pltpu.make_async_copy(slab_any.at[here], slab_ref.at[here], sems.at[p]))
        copies[p].start()
    for p in range(2):
        copies[p].wait()
        slabs = jnp.concatenate(
            [slab_ref[p * share : (p + 1) * share, c].reshape(share * states, width) for c in range(homes)], axis=1
        )
        part = jnp.dot(
            weights_ref[:, p * share * states : (p + 1) * share * states], slabs, preferred_element_type=F32
        )
        if p == 0:
            total_ref[...] = part
        else:
            density_ref[...] = (total_ref[...] + part).astype(BF16)
    row = lax.broadcasted_iota(jnp.int32, (half, width), 0)
    lane = lax.broadcasted_iota(jnp.int32, (half, width), 1)
    masks = [lane == row + half * k for k in range(2)]
    slim = lax.broadcasted_iota(jnp.int32, (8, width), 0)
    for h in range(homes):
        c = FIRST[h]
        product = jnp.dot(change_ref[c], density_ref[:, h * width : (h + 1) * width], preferred_element_type=F32)
        product = product.reshape(2, 3, half, width)
        force = jnp.zeros((8, width), F32)
        for x in range(3):
            kept = jnp.where(masks[0], product[0, x], 0.0) + jnp.where(masks[1], product[1, x], 0.0)
            force = jnp.where(slim == x, jnp.sum(kept, axis=0, keepdims=True), force)
        high = force.astype(BF16).astype(F32)
        out_ref[RETURN[c]] = jnp.concatenate([high, force - high], axis=0).astype(BF16)


def hot_kernel(owner_ref, atom_ref, out_ref, rows_ref):
    columns, width, atoms = out_ref.shape
    blocks = owner_ref.shape[0]
    half = width // 2
    lane = lax.broadcasted_iota(jnp.int32, (1, width), 1)
    rows_ref[...] = jnp.full(rows_ref.shape, -1, jnp.int32)
    for b in range(blocks):
        o = owner_ref[b]
        rank = jnp.int32(0)
        for earlier in range(b):
            rank = rank + (owner_ref[earlier] == o).astype(jnp.int32)

        @pl.when(o >= 0)
        def _():
            here = rows_ref[pl.ds(o, 1), :]
            rows_ref[pl.ds(o, 1), :] = jnp.where(lane // half == rank, atom_ref[b : b + 1, :], here)

    atom = lax.broadcasted_iota(jnp.int32, (atoms, width), 0)
    for o in range(columns):
        hot = (atom == rows_ref[o : o + 1, :]).astype(F32)
        out_ref[o] = hot.T.astype(BF16)


def gather_kernel(force_ref, hot_ref, out_ref):
    columns = force_ref.shape[0]
    total = jnp.zeros((force_ref.shape[1], hot_ref.shape[2]), F32)
    for o in range(columns):
        total = total + jnp.dot(force_ref[RETURN[o]], hot_ref[o], preferred_element_type=F32)
    out_ref[...] = 2.0 * (total[0:3, : out_ref.shape[1]] + total[8:11, : out_ref.shape[1]])


def per_device(
    eigvec_slab, occupations, energies, tile_owner, margin_change, hamiltonian_change, basis_atom
):
    columns = lax.axis_size("col")
    rows = lax.axis_size("row")
    col_index = lax.axis_index("col")
    row_index = lax.axis_index("row")
    states = eigvec_slab.shape[0]
    blocks = tile_owner.shape[0]
    block_rows = margin_change.shape[2]
    width = margin_change.shape[3]

    def swap(x, groups=None):
        return lax.all_to_all(x, "col", split_axis=0, concat_axis=0, tiled=True, axis_index_groups=groups)

    announced = pl.pallas_call(
        announce_kernel,
        grid=(1,),
        in_specs=[whole(SMEM), pl.BlockSpec((states, width), lambda i: (0, 0))],
        out_specs=pl.BlockSpec((columns, states + 16, width), lambda i: (0, 0, 0)),
        out_shape=jax.ShapeDtypeStruct((columns, states + 16, width), BF16),
    )(tile_owner, eigvec_slab)
    heard = swap(announced, [list(FIRST)])
    heard, slab = lax.optimization_barrier((heard, eigvec_slab))
    table = heard[:, states, : 2 * columns].astype(jnp.int32)
    packed_shape = (columns, columns, states, width)
    packed = pl.pallas_call(
        pack_kernel,
        in_specs=[whole(pl.ANY), whole()],
        out_specs=whole(pl.ANY),
        out_shape=jax.ShapeDtypeStruct(packed_shape, BF16),
        scratch_shapes=[
            pltpu.SMEM(table.shape, jnp.int32),
            pltpu.VMEM((columns, blocks + 1, states, width), BF16),
            pltpu.VMEM(packed_shape, BF16),
            pltpu.SemaphoreType.DMA((columns + 1,)),
        ],
        compiler_params=pltpu.CompilerParams(vmem_limit_bytes=16 << 20),
    )(table, slab)
    slabs = swap(packed)

    panel = heard[:, :states, :]
    panel = jnp.where(row_index == 0, panel, jnp.zeros_like(panel))
    reach = 1
    while reach < rows:
        panel = panel + lax.ppermute(panel, "row", [(i, i + reach) for i in range(reach)])
        reach *= 2
    occ = occupations.astype(F32)
    eweight = occ * energies
    weights = pl.pallas_call(
        weights_kernel,
        in_specs=[whole(), whole()],
        out_specs=whole(),
        out_shape=jax.ShapeDtypeStruct((2 * width, columns * states), BF16),
        cost_estimate=pl.CostEstimate(flops=1 << 20, bytes_accessed=1 << 19, transcendentals=0),
        compiler_params=pltpu.CompilerParams(vmem_limit_bytes=8 << 20),
    )(panel, jnp.stack([occ, -eweight]))

    weights, ham, margin, owner = lax.optimization_barrier(
        (weights, hamiltonian_change, margin_change, tile_owner)
    )

    device = row_index * columns + col_index
    atom = lax.dynamic_slice_in_dim(basis_atom, device * blocks * block_rows, blocks * block_rows)
    atom = (atom - device * ATOMS_DEV).reshape(blocks, block_rows)
    atom = jnp.concatenate([atom, atom], axis=1)
    atoms_padded = -(-ATOMS_DEV // 128) * 128
    hot = pl.pallas_call(
        hot_kernel,
        in_specs=[whole(SMEM), whole()],
        out_specs=whole(),
        out_shape=jax.ShapeDtypeStruct((columns, width, atoms_padded), BF16),
        scratch_shapes=[pltpu.VMEM((columns, width), jnp.int32)],
        cost_estimate=pl.CostEstimate(flops=4 << 20, bytes_accessed=1 << 20, transcendentals=0),
        compiler_params=pltpu.CompilerParams(vmem_limit_bytes=8 << 20),
    )(owner, atom)

    change = pl.pallas_call(
        change_kernel,
        in_specs=[whole(), whole()],
        out_specs=whole(),
        out_shape=jax.ShapeDtypeStruct((columns, 6 * block_rows, 2 * width), BF16),
        cost_estimate=pl.CostEstimate(flops=1 << 20, bytes_accessed=6 << 20, transcendentals=0),
        compiler_params=pltpu.CompilerParams(vmem_limit_bytes=16 << 20),
    )(ham, margin)
    slabs, weights, change, hot = lax.optimization_barrier((slabs, weights, change, hot))
    force = pl.pallas_call(
        owner_kernel,
        in_specs=[whole(pl.ANY), whole(), whole()],
        out_specs=whole(),
        out_shape=jax.ShapeDtypeStruct((columns, 16, width), BF16),
        scratch_shapes=[
            pltpu.VMEM(slabs.shape, BF16),
            pltpu.VMEM((2 * width, columns * width), F32),
            pltpu.VMEM((2 * width, columns * width), BF16),
            pltpu.SemaphoreType.DMA((2,)),
        ],
        compiler_params=pltpu.CompilerParams(vmem_limit_bytes=16 << 20),
    )(slabs, weights, change)

    returned = swap(force, [list(BACK)])
    return pl.pallas_call(
        gather_kernel,
        in_specs=[whole(), whole()],
        out_specs=whole(),
        out_shape=jax.ShapeDtypeStruct((3, ATOMS_DEV), F32),
        compiler_params=pltpu.CompilerParams(vmem_limit_bytes=8 << 20),
    )(returned, hot)


def solution(mesh):
    return jax.shard_map(
        per_device,
        mesh=mesh,
        in_specs=(
            P("col", "row"),
            P(),
            P(),
            P(("row", "col")),
            P(("row", "col"), None, None, None),
            P(("row", "col"), None, None, None),
            P(),
        ),
        out_specs=P(None, ("row", "col")),
        check_vma=False,
    )
```
